512 devices in a mesh: field: 32 (over x, y), cap: 4 (over z_lo, core), bank: 4 (over z_hi).
Axes of the slice: x: 4, y: 8, z: 8 (z_hi: 4, z_lo: 2; z = z_hi * 2 + z_lo), core: 2. Of those that a mesh axis runs over, the one named last changes fastest.
Arguments:
- pattern: bfloat16 [4, 3, 542, 8192], P('cap', None, None, 'field'), may hold values from -6 to 6
- measured: bfloat16 [4, 3, 32, 8192], P('cap', None, None, 'field'), may hold values from -6 to 6
- row_kernels: bfloat16 [64, 3, 16, 511], P('field', None, 'bank'), may hold values from -0.125 to 0.125
- col_kernels: bfloat16 [64, 3, 16, 511], P('field', None, 'bank'), may hold values from -0.125 to 0.125
- tile_patch: int32 [64], P('field'), may hold values from 0 to 1
- sat_tiles: int32 [4, 256], P('cap'), may hold values from 0 to 1023
Outputs:
- grad_rows: float32 [64, 3, 16, 511], P('field', None, 'bank')
- grad_cols: float32 [64, 3, 16, 511], P('field', None, 'bank')
The draws below stay inside these ranges and needn't reach their ends.
Inputs may be any that keep to these rules, and one draw needn't show every extreme that they name: Patch t of the window uses kernel set (t // 2) * 2 + tile_patch[t]. `sat_tiles`: tile numbers run row by row over tiles of 16 x 16 pixels of the window; an entry may repeat.
All inputs are finite; a program needn't handle non-finite values.
Results may differ from the reference program's by a relative error of at most 0.0033.
Values may be sent and summed in bfloat16 or wider, within the bound.
A program may use at most 64 MiB of HBM per device.

```python
import math
import jax
import jax.numpy as jnp
import numpy as np
from jax import lax

TAPS = 511
RANKS = 16
COLOURS = 3
PW = 128
PATCH_DEV = 2
H = 32
TILE = 16
NSAT = 256
HALF = 255
R = 542
NX = 8192
NPATCH = 64
CAPS = 4
NTILES = 1024


def plant(drawn, rng, least, high):
    longest = drawn.shape.index(max(drawn.shape))
    spots = []
    for shift in (0, 1):
        where = [jax.random.randint(jax.random.fold_in(rng, axis), (), 0, length) for axis, length in enumerate(drawn.shape)]
        where[longest] = (where[longest] + shift) % drawn.shape[longest]
        spots.append(tuple(where))
    return drawn.at[spots[0]].set(least).at[spots[1]].set(high)


def levels(key, dims, cuts, least, top_value):
    def one(axis_at, blocks):
        draws = jax.random.uniform(jax.random.fold_in(jax.random.fold_in(key, 6), axis_at), (blocks,), jnp.float32, least / len(cuts), top_value / len(cuts))
        return jnp.repeat(jnp.exp(draws), dims[axis_at] // blocks).reshape((-1,) + (1,) * (len(dims) - axis_at - 1))

    loudness = one(*cuts[0])
    for cut in cuts[1:]:
        loudness = loudness * one(*cut)
    return loudness


def rank_bounds(amount, skew):
    portions = [(1 << 20) // math.isqrt(standing ** skew) + 1 for standing in range(1, amount + 1)]
    width = 1 + sum(portions) // (1 << 30)
    return np.cumsum(np.array([max(1, weight // width) for weight in portions]))


def skewed_ids(own_key, shape, count, lean):
    listing = rank_bounds(count, lean)
    ticket = jax.random.randint(jax.random.fold_in(own_key, 1), shape, 0, int(listing[count - 1]))
    rank = jnp.searchsorted(jnp.asarray(listing, jnp.int32), ticket, side="right")
    return jax.random.permutation(jax.random.fold_in(own_key, 2), count)[rank].astype(jnp.int32)


def bell_draw(key, extent, scale, limit, pieces=(), kind=jnp.bfloat16):
    drawn = scale * jax.random.normal(key, extent, jnp.float32)
    if pieces:
        drawn = drawn * levels(key, extent, pieces, -0.22, 0.18)
    return jnp.clip(drawn, -limit, limit).astype(kind)


def setup_inputs(seed: int = 0) -> dict:
    streams_of = jax.random.split(jax.random.key(seed), 7)
    return {
        "pattern": bell_draw(streams_of[0], (CAPS, COLOURS, R, NX), 1.0, 6.0, ((0, 4), (3, 32))),
        "measured": bell_draw(streams_of[1], (CAPS, COLOURS, H, NX), 1.0, 6.0, ((0, 4), (3, 32))),
        "row_kernels": bell_draw(streams_of[2], (NPATCH, COLOURS, RANKS, TAPS), (4 * TAPS) ** -0.5, 0.125, ((0, 32), (2, 4))),
        "col_kernels": bell_draw(streams_of[3], (NPATCH, COLOURS, RANKS, TAPS), (4 * TAPS) ** -0.5, 0.125, ((0, 32), (2, 4))),
        "tile_patch": plant(jax.random.randint(streams_of[4], (NPATCH,), 0, PATCH_DEV), jax.random.fold_in(streams_of[4], 1), 0, PATCH_DEV - 1).astype(jnp.int32),
        "sat_tiles": plant(skewed_ids(streams_of[5], (CAPS, NSAT), NTILES, 2), jax.random.fold_in(streams_of[5], 3), 0, NTILES - 1).astype(jnp.int32),
    }


def banded(kernel, band_width):
    tap_count = kernel.shape[-1]
    span_len = band_width + tap_count - 1
    zero_tail = jnp.zeros(kernel.shape[:-1] + (band_width,), kernel.dtype)
    padded = jnp.concatenate([kernel, zero_tail], axis=-1)
    repeated = jnp.tile(padded, (1,) * (kernel.ndim - 1) + (band_width,))
    return repeated[..., : band_width * span_len].reshape(kernel.shape[:-1] + (band_width, span_len))


def diagonals(matrix, tap_count):
    line_count = matrix.shape[-2]
    span_len = matrix.shape[-1]
    flattened = matrix.reshape(matrix.shape[:-2] + (line_count * span_len,))
    zero_tail = jnp.zeros(matrix.shape[:-2] + (line_count,), matrix.dtype)
    flattened = jnp.concatenate([flattened, zero_tail], axis=-1)
    shaped = flattened.reshape(matrix.shape[:-2] + (line_count, span_len + 1))
    return jnp.sum(shaped[..., :tap_count], axis=-2)


def reference(pattern, measured, row_kernels, col_kernels, tile_patch, sat_tiles):
    extended = jnp.pad(pattern, ((0, 0), (0, 0), (0, 0), (HALF, HALF)))
    tile_ids = (jnp.arange(H // TILE, dtype=jnp.int32)[:, None] * (NX // TILE)
                + jnp.arange(NX // TILE, dtype=jnp.int32)[None, :]).astype(jnp.int32)
    saturated = jnp.any(tile_ids[None, :, :, None] == sat_tiles[:, None, None, :], axis=-1)
    keep_tiles = 1.0 - saturated.astype(jnp.float32)
    keep_pixels = jnp.broadcast_to(keep_tiles[:, :, None, :, None],
                                   (CAPS, H // TILE, TILE, NX // TILE, TILE)).reshape(CAPS, H, NX)
    patch_ids = jnp.arange(NPATCH, dtype=jnp.int32)
    kernel_sets = ((patch_ids // PATCH_DEV) * PATCH_DEV + tile_patch).astype(jnp.int32)

    def one_tile(tile_index):
        chosen = kernel_sets[tile_index]
        row_taps = row_kernels[chosen]
        col_taps = col_kernels[chosen]
        start = (tile_index * PW).astype(jnp.int32)
        window_cols = lax.dynamic_slice_in_dim(extended, start, PW + 2 * HALF, 3).astype(jnp.float32)
        row_band = banded(row_taps, PW).astype(jnp.float32)
        col_band = banded(col_taps, H).astype(jnp.float32)
        rowpass = jnp.einsum("cqyj,qrxj->cqryx", window_cols, row_band).astype(jnp.bfloat16)
        rowpass_wide = rowpass.astype(jnp.float32)
        predicted = jnp.einsum("qryk,cqrkx->cqyx", col_band, rowpass_wide)
        measured_tile = lax.dynamic_slice_in_dim(measured, start, PW, 3).astype(jnp.float32)
        keep_tile = lax.dynamic_slice_in_dim(keep_pixels, start, PW, 2)
        residual = (keep_tile[:, None] * (predicted - measured_tile)).astype(jnp.bfloat16)
        residual_wide = residual.astype(jnp.float32)
        backward = jnp.einsum("qryk,cqyx->cqrkx", col_band, residual_wide).astype(jnp.bfloat16)
        row_terms = jnp.einsum("cqrkx,cqkj->qrxj", backward.astype(jnp.float32), window_cols)
        col_terms = jnp.einsum("cqyx,cqrkx->qryk", residual_wide, rowpass_wide)
        return diagonals(row_terms, TAPS), diagonals(col_terms, TAPS)

    per_row, per_col = lax.map(one_tile, patch_ids)
    grad_rows = jax.ops.segment_sum(per_row, kernel_sets, num_segments=NPATCH) * (1.0 / H)
    grad_cols = jax.ops.segment_sum(per_col, kernel_sets, num_segments=NPATCH) * (1.0 / H)
    return grad_rows, grad_cols
```

```python
import functools

import jax
import jax.numpy as jnp
from jax import lax
from jax.experimental import pallas as pl
from jax.experimental.pallas import tpu as pltpu
from jax.sharding import PartitionSpec as P

TILE = 16
PW = 128
BF = jnp.bfloat16
F32 = jnp.float32
MESH = pl.DeviceIdType.MESH

SPAN = ((0, 128), (0, 256), (0, 256), (0, 256), (0, 256), (128, 128))


def nt(a, b):
    return lax.dot_general(a, b, (((1,), (1,)), ((), ())), preferred_element_type=F32)


def nn(a, b):
    return jnp.dot(a, b, preferred_element_type=F32)


def flip(rows, block):
    i = lax.broadcasted_iota(jnp.int32, (rows, rows), 0)
    j = lax.broadcasted_iota(jnp.int32, (rows, rows), 1)
    same = (i // block) == (j // block)
    return (same & ((i % block) + (j % block) == block - 1)).astype(F32).astype(BF)


def kernel(
    fields, banks, caps, across,
    tile_ref, sat_ref, meas_ref, rowk_ref, colk_ref, pat_hbm,
    out_row, out_col,
    pat, k3, kf, tb, cb, cp, s1, f1, s2, f2, rs, rb, ct, gc, gp, gn, ga,
    pat_sem, k_s, k_r, f1_s, f1_r, f2_s, f2_r, r_s, r_r, g_s, g_r, c_s, c_r,
):
    colours, ranks = 3, 4
    rows_ext = pat.shape[1]
    span = rows_ext - TILE
    me_f = lax.axis_index("field")
    me_b = lax.axis_index("bank")
    me_c = lax.axis_index("cap")
    side_f = (lax.rem(me_f + fields - 1, fields), me_f, lax.rem(me_f + 1, fields))
    bank_at = [lax.rem(me_b + k, banks) for k in range(banks)]
    cap_at = [lax.rem(me_c + k, caps) for k in range(caps)]

    load = pltpu.make_async_copy(pat_hbm.at[0], pat, pat_sem)
    load.start()

    barrier = pltpu.get_barrier_semaphore()
    peers = 0
    for s in range(3):
        for k in range(banks):
            if s != 1 or k != 0:
                pl.semaphore_signal(
                    barrier, inc=1, device_id={"field": side_f[s], "bank": bank_at[k]}, device_id_type=MESH
                )
                peers += 1
    for k in range(1, caps):
        pl.semaphore_signal(barrier, inc=1, device_id={"cap": cap_at[k]}, device_id_type=MESH)
        peers += 1

    uses_one = [tile_ref[t] == 1 for t in range(2)]
    k3[1] = jnp.zeros((48, 512), BF)
    for kind, ref in ((0, rowk_ref), (1, colk_ref)):
        for t in range(2):
            for q in range(colours):
                at = ((kind * 2 + t) * colours + q) * ranks
                first = ref[0, q].astype(F32)
                second = ref[1, q].astype(F32)
                k3[1, at : at + ranks, 0:511] = jnp.where(uses_one[t], second, first).astype(BF)

    pl.semaphore_wait(barrier, peers)
    k_copies = []
    for i, s in enumerate((0, 2)):
        copy = pltpu.make_async_remote_copy(
            src_ref=k3.at[1], dst_ref=k3.at[2 - s], send_sem=k_s.at[i], recv_sem=k_r.at[1 - i],
            device_id={"field": side_f[s]}, device_id_type=MESH,
        )
        copy.start()
        k_copies.append(copy)

    gp[...] = jnp.zeros(gp.shape, F32)
    rb[...] = jnp.zeros(rb.shape, BF)
    ct[...] = jnp.zeros(ct.shape, F32)

    row_half = me_b // 2
    patch_half = lax.rem(me_b, 2)
    first_tile = row_half * across + me_f * (2 * PW // TILE) + patch_half * (PW // TILE)
    sub = lax.broadcasted_iota(jnp.int32, (8, sat_ref.shape[1]), 0)
    hit = (jnp.broadcast_to(sat_ref[0:1, :], (8, sat_ref.shape[1])) == sub + first_tile).astype(F32)
    hit = jnp.max(hit, axis=1, keepdims=True)
    lane_tile = lax.broadcasted_iota(jnp.int32, (8, PW), 1) // TILE
    mine = (lane_tile == lax.broadcasted_iota(jnp.int32, (8, PW), 0)).astype(F32)
    keep = 1.0 - jnp.sum(hit * mine, axis=0, keepdims=True)

    def bands(s):
        taps = k3[s].astype(F32)
        if s == 0:
            taps = taps * (me_f > 0).astype(F32)
        if s == 2:
            taps = taps * (me_f < fields - 1).astype(F32)
        kf[s] = jnp.zeros((48, 1024), F32)
        kf[s, 0:24, 256:768] = pltpu.roll(taps[0:24], 1, 1)
        kf[s, 24:48, 0:512] = taps[24:48]
        for t in range(2):
            p = 2 * s + t
            j0, jw = SPAN[p]
            for q in range(colours):
                for r in range(ranks):
                    at = (t * colours + q) * ranks + r
                    off = 256 + 128 * (3 - p)
                    line = jnp.broadcast_to(kf[s, at : at + 1, off + j0 : off + j0 + 128 + jw], (PW, 128 + jw))
                    tilted = pltpu.roll(line, 0, 1, stride=1, stride_axis=0)
                    tb[q, p, :, r * jw : (r + 1) * jw] = tilted[:, 128:].astype(BF)
                    line = jnp.broadcast_to(kf[s, 24 + at : 25 + at, 0:640], (TILE, 640))
                    tilted = pltpu.roll(line, 0, 1, stride=1, stride_axis=0)
                    at = (p * ranks + r) * TILE
                    cb[q, at : at + TILE, :] = tilted.astype(BF)

    bands(1)
    for i, s in enumerate((0, 2)):
        pltpu.make_async_remote_copy(
            src_ref=k3.at[1], dst_ref=k3.at[s], send_sem=k_s.at[i], recv_sem=k_r.at[i],
            device_id={"field": side_f[s]}, device_id_type=MESH,
        ).wait_recv()
        bands(s)
    load.wait()

    sends = list(k_copies)

    def forward(q):
        for u in range(2):
            passed = nn(cb[q, :, 0:span], pat[q, u * TILE : u * TILE + span, :]).astype(BF)
            for p in range(6):
                j0, jw = SPAN[p]
                for r in range(ranks):
                    at = (p * ranks + r) * TILE
                    cp[q, p, u * TILE : (u + 1) * TILE, r * jw : (r + 1) * jw] = passed[at : at + TILE, j0 : j0 + jw]
        for s in (0, 2, 1):
            for t in range(2):
                p = 2 * s + t
                wide = ranks * SPAN[p][1]
                part = nt(cp[q, p, :, 0:wide], tb[q, p, :, 0:wide])
                for h in range(2):
                    s1[q, s, h * 2 + t] = part[h * TILE : (h + 1) * TILE]
            if s != 1:
                i = s // 2
                copy = pltpu.make_async_remote_copy(
                    src_ref=s1.at[q, s], dst_ref=f1.at[q, 1 - i], send_sem=f1_s.at[q, i], recv_sem=f1_r.at[q, 1 - i],
                    device_id={"field": side_f[s]}, device_id_type=MESH,
                )
                copy.start()
                sends.append(copy)

    def mid_one(q):
        for i in range(2):
            pltpu.make_async_remote_copy(
                src_ref=s1.at[q, 1], dst_ref=f1.at[q, i], send_sem=f1_s.at[q, i], recv_sem=f1_r.at[q, i],
                device_id={"field": side_f[2 * i]}, device_id_type=MESH,
            ).wait_recv()
        s2[q] = s1[q, 1] + f1[q, 0] + f1[q, 1]
        for k in range(1, banks):
            copy = pltpu.make_async_remote_copy(
                src_ref=s2.at[q, bank_at[k]], dst_ref=f2.at[q, banks - k],
                send_sem=f2_s.at[q, k], recv_sem=f2_r.at[q, banks - k],
                device_id={"bank": bank_at[k]}, device_id_type=MESH,
            )
            copy.start()
            sends.append(copy)

    def mid_two(q):
        total = s2[q, me_b]
        for k in range(1, banks):
            pltpu.make_async_remote_copy(
                src_ref=s2.at[q, 0], dst_ref=f2.at[q, k], send_sem=f2_s.at[q, k], recv_sem=f2_r.at[q, k],
                device_id={"bank": bank_at[k]}, device_id_type=MESH,
            ).wait_recv()
            total = total + f2[q, k]
        seen = meas_ref[0, q, pl.ds(row_half * TILE, TILE), pl.ds(patch_half * PW, PW)].astype(F32)
        rs[q, 1, me_b] = (keep * (total - seen)).astype(BF)
        for s in range(3):
            for k in range(banks):
                if s == 1 and k == 0:
                    continue
                copy = pltpu.make_async_remote_copy(
                    src_ref=rs.at[q, 1, me_b], dst_ref=rs.at[q, 2 - s, me_b],
                    send_sem=r_s.at[q, s, k], recv_sem=r_r.at[q, 2 - s, (banks - k) % banks],
                    device_id={"field": side_f[s], "bank": bank_at[k]}, device_id_type=MESH,
                )
                copy.start()
                sends.append(copy)

    def backward(q):
        for s in range(3):
            for k in range(banks):
                if s == 1 and k == 0:
                    continue
                pltpu.make_async_remote_copy(
                    src_ref=rs.at[q, 1, me_b], dst_ref=rs.at[q, s, bank_at[k]],
                    send_sem=r_s.at[q, s, k], recv_sem=r_r.at[q, s, k],
                    device_id={"field": side_f[s], "bank": bank_at[k]}, device_id_type=MESH,
                ).wait_recv()
        for p in range(6):
            s, t = p // 2, p % 2
            j0, jw = SPAN[p]
            wide = ranks * jw
            res = jnp.concatenate([rs[q, s, t], rs[q, s, 2 + t]], axis=0)
            turned = nn(flip(2 * TILE, TILE), res).astype(BF)
            across_x = nt(flip(PW, PW), res).astype(BF)
            back = nn(turned, tb[q, p, :, 0:wide]).astype(BF)
            for u in range(2):
                for r in range(ranks):
                    at = (p * ranks + r) * TILE
                    rb[u, at : at + TILE, j0 : j0 + jw] = back[u * TILE : (u + 1) * TILE, r * jw : (r + 1) * jw]
            for r in range(ranks):
                terms = nn(across_x, cp[q, p, :, r * jw : (r + 1) * jw])
                terms = jnp.concatenate([terms, jnp.zeros((PW, 128), F32)], axis=1)
                tilted = pltpu.roll(terms, 0, 1, stride=1, stride_axis=0)
                line = jnp.sum(tilted, axis=0, keepdims=True)
                low = 128 * (3 - p) + j0
                skip = max(0, -low)
                stop = min(128 + jw, 512 - low)
                at = t * ranks + r
                gp[q, s, at : at + 1, low + skip : low + stop] = line[:, skip:stop]
        ct[:, 0:span] = nt(rb[0], pat[q, 0:span, :]) + nt(rb[1], pat[q, TILE : TILE + span, :])
        for p in range(6):
            for r in range(ranks):
                at = p * ranks + r
                tilted = pltpu.roll(ct[at * TILE : (at + 1) * TILE, :], 0, 1, stride=1, stride_axis=0)
                gc[at : at + 1, :] = jnp.sum(tilted, axis=0, keepdims=True)
        lines = pltpu.roll(gc[...], 640 - (TILE - 1), 1)[:, 0:512]
        for s in range(3):
            gp[q, s, 8:16, :] = lines[8 * s : 8 * s + 8]
        for i, s in enumerate((0, 2)):
            copy = pltpu.make_async_remote_copy(
                src_ref=gp.at[q, s], dst_ref=gn.at[q, 1 - i], send_sem=g_s.at[q, i], recv_sem=g_r.at[q, 1 - i],
                device_id={"field": side_f[s]}, device_id_type=MESH,
            )
            copy.start()
            sends.append(copy)

    one = [jnp.where(u, 1.0, 0.0) for u in uses_one]

    def tail_one(q):
        for i in range(2):
            pltpu.make_async_remote_copy(
                src_ref=gp.at[q, 1], dst_ref=gn.at[q, i], send_sem=g_s.at[q, i], recv_sem=g_r.at[q, i],
                device_id={"field": side_f[2 * i]}, device_id_type=MESH,
            ).wait_recv()
        total = gp[q, 1] + gn[q, 0] + gn[q, 1]
        for kind in range(2):
            a = total[8 * kind : 8 * kind + 4]
            b = total[8 * kind + 4 : 8 * kind + 8]
            ga[q, me_c, 8 * kind : 8 * kind + 4] = a * (1.0 - one[0]) + b * (1.0 - one[1])
            ga[q, me_c, 8 * kind + 4 : 8 * kind + 8] = a * one[0] + b * one[1]
        for k in range(1, caps):
            copy = pltpu.make_async_remote_copy(
                src_ref=ga.at[q, me_c], dst_ref=ga.at[q, me_c], send_sem=c_s.at[q, k], recv_sem=c_r.at[q, caps - k],
                device_id={"cap": cap_at[k]}, device_id_type=MESH,
            )
            copy.start()
            sends.append(copy)

    def tail_two(q):
        for k in range(1, caps):
            pltpu.make_async_remote_copy(
                src_ref=ga.at[q, me_c], dst_ref=ga.at[q, cap_at[k]], send_sem=c_s.at[q, k], recv_sem=c_r.at[q, k],
                device_id={"cap": cap_at[k]}, device_id_type=MESH,
            ).wait_recv()
        total = ga[q, 0]
        for c in range(1, caps):
            total = total + ga[q, c]
        total = total * (1.0 / 32)
        for k in range(2):
            out_row[k, q] = total[4 * k : 4 * k + 4, 0:511]
            out_col[k, q] = total[8 + 4 * k : 12 + 4 * k, 0:511]

    forward(0)
    forward(1)
    mid_one(0)
    forward(2)
    mid_two(0)
    mid_one(1)
    mid_two(1)
    mid_one(2)
    backward(0)
    mid_two(2)
    backward(1)
    tail_one(0)
    backward(2)
    tail_one(1)
    tail_two(0)
    tail_one(2)
    tail_two(1)
    tail_two(2)
    for copy in sends:
        copy.wait_send()


def body(pattern, measured, row_kernels, col_kernels, tile_patch, sat_tiles):
    fields, banks, caps = (lax.axis_size(a) for a in ("field", "bank", "cap"))
    _, colours, rows_ext, strip = pattern.shape
    across = fields * strip // TILE
    vm = pl.BlockSpec(memory_space=pltpu.VMEM)
    dma = pltpu.SemaphoreType.DMA
    out = jax.ShapeDtypeStruct(row_kernels.shape, F32)
    return pl.pallas_call(
        functools.partial(kernel, fields, banks, caps, across),
        out_shape=(out, out),
        in_specs=[pl.BlockSpec(memory_space=pltpu.SMEM), vm, vm, vm, vm, pl.BlockSpec(memory_space=pl.ANY)],
        out_specs=(vm, vm),
        scratch_shapes=[
            pltpu.VMEM((colours, rows_ext, strip), BF),
            pltpu.VMEM((3, 48, 512), BF),
            pltpu.VMEM((3, 48, 1024), F32),
            pltpu.VMEM((colours, 6, PW, 1024), BF),
            pltpu.VMEM((colours, 384, 640), BF),
            pltpu.VMEM((colours, 6, 32, 1024), BF),
            pltpu.VMEM((colours, 3, 4, TILE, PW), F32),
            pltpu.VMEM((colours, 2, 4, TILE, PW), F32),
            pltpu.VMEM((colours, 4, TILE, PW), F32),
            pltpu.VMEM((colours, 4, TILE, PW), F32),
            pltpu.VMEM((colours, 3, 4, TILE, PW), BF),
            pltpu.VMEM((2, 384, strip), BF),
            pltpu.VMEM((384, 640), F32),
            pltpu.VMEM((24, 640), F32),
            pltpu.VMEM((colours, 3, 16, 512), F32),
            pltpu.VMEM((colours, 2, 16, 512), F32),
            pltpu.VMEM((colours, caps, 16, 512), F32),
            dma, dma((2,)), dma((2,)), dma((colours, 2)), dma((colours, 2)),
            dma((colours, banks)), dma((colours, banks)), dma((colours, 3, banks)), dma((colours, 3, banks)),
            dma((colours, 2)), dma((colours, 2)), dma((colours, caps)), dma((colours, caps)),
        ],
        compiler_params=pltpu.CompilerParams(
            collective_id=0, has_side_effects=True, vmem_limit_bytes=40 << 20
        ),
    )(tile_patch, sat_tiles, measured, row_kernels, col_kernels, pattern)


def solution(mesh):
    return jax.shard_map(
        body,
        mesh=mesh,
        in_specs=(
            P("cap", None, None, "field"),
            P("cap", None, None, "field"),
            P("field", None, "bank", None),
            P("field", None, "bank", None),
            P("field"),
            P("cap", None),
        ),
        out_specs=(P("field", None, "bank", None), P("field", None, "bank", None)),
        check_vma=False,
    )
```

```python
import functools

import jax
import jax.numpy as jnp
from jax import lax
from jax.experimental import pallas as pl
from jax.experimental.pallas import tpu as pltpu
from jax.sharding import PartitionSpec as P

TILE = 16
PW = 128
BF = jnp.bfloat16
F32 = jnp.float32
MESH = pl.DeviceIdType.MESH

SPAN = ((0, 128), (0, 256), (0, 256), (0, 256), (0, 256), (128, 128))


def nt(a, b):
    return lax.dot_general(a, b, (((1,), (1,)), ((), ())), preferred_element_type=F32)


def nn(a, b):
    return jnp.dot(a, b, preferred_element_type=F32)


def flip(rows, block):
    i = lax.broadcasted_iota(jnp.int32, (rows, rows), 0)
    j = lax.broadcasted_iota(jnp.int32, (rows, rows), 1)
    same = (i // block) == (j // block)
    return (same & ((i % block) + (j % block) == block - 1)).astype(F32).astype(BF)


def kernel(
    fields, banks, caps, across,
    tile_hbm, sat_hbm, meas_hbm, rowk_hbm, colk_hbm, pat_hbm,
    out_row, out_col,
    tile_ref, sat, meas, rowk, colk, pat,
    k3, kf, tb, cb, cp, own, f1s, f1, f2s, f2, rs, rb, ct, gc, gp, gn, ga,
    in_sem, k_s, k_r, f1_s, f1_r, f2_s, f2_r, r_s, r_r, g_s, g_r, c_s, c_r,
):
    colours, ranks = 3, 4
    rows_ext = pat.shape[1]
    span = rows_ext - TILE
    me_f = lax.axis_index("field")
    me_b = lax.axis_index("bank")
    me_c = lax.axis_index("cap")
    side_f = (lax.rem(me_f + fields - 1, fields), me_f, lax.rem(me_f + 1, fields))
    bank_at = [lax.rem(me_b + k, banks) for k in range(banks)]
    cap_at = [lax.rem(me_c + k, caps) for k in range(caps)]

    barrier = pltpu.get_barrier_semaphore()
    for k in (2, 1, 3):
        pl.semaphore_signal(barrier, inc=1, device_id={"bank": bank_at[k]}, device_id_type=MESH)
    for s in (0, 2):
        pl.semaphore_signal(barrier, inc=1, device_id={"field": side_f[s]}, device_id_type=MESH)
    for k in range(1, caps):
        pl.semaphore_signal(barrier, inc=1, device_id={"cap": cap_at[k]}, device_id_type=MESH)

    loads = [
        pltpu.make_async_copy(src, dst, in_sem.at[i])
        for i, (src, dst) in enumerate(
            ((tile_hbm, tile_ref), (rowk_hbm, rowk), (colk_hbm, colk), (sat_hbm, sat), (pat_hbm.at[0], pat), (meas_hbm.at[0], meas))
        )
    ]
    for load in loads:
        load.start()

    gp[...] = jnp.zeros(gp.shape, F32)
    rb[...] = jnp.zeros(rb.shape, BF)
    ct[...] = jnp.zeros(ct.shape, F32)
    k3[1] = jnp.zeros((48, 512), BF)
    kf[...] = jnp.zeros(kf.shape, F32)

    for load in loads[0:4]:
        load.wait()
    uses_one = [tile_ref[t] == 1 for t in range(2)]
    for kind, ref in ((0, rowk), (1, colk)):
        for t in range(2):
            for q in range(colours):
                at = ((kind * 2 + t) * colours + q) * ranks
                first = ref[0, q].astype(F32)
                second = ref[1, q].astype(F32)
                k3[1, at : at + ranks, 0:511] = jnp.where(uses_one[t], second, first).astype(BF)

    pl.semaphore_wait(barrier, 2 + banks - 1 + caps - 1)
    sends = []
    for i, s in enumerate((0, 2)):
        copy = pltpu.make_async_remote_copy(
            src_ref=k3.at[1], dst_ref=k3.at[2 - s], send_sem=k_s.at[i], recv_sem=k_r.at[1 - i],
            device_id={"field": side_f[s]}, device_id_type=MESH,
        )
        copy.start()
        sends.append(copy)

    tiles = 2 * PW // TILE
    sub = lax.broadcasted_iota(jnp.int32, (tiles, sat.shape[1]), 0)
    listed = jnp.broadcast_to(sat[0:1, :], (tiles, sat.shape[1]))
    lane_tile = lax.broadcasted_iota(jnp.int32, (tiles, 2 * PW), 1) // TILE
    mine = (lane_tile == lax.broadcasted_iota(jnp.int32, (tiles, 2 * PW), 0)).astype(F32)
    keep = []
    for h in range(2):
        hit = (listed == sub + (h * across + me_f * tiles)).astype(F32)
        hit = jnp.max(hit, axis=1, keepdims=True)
        line = 1.0 - jnp.sum(hit * mine, axis=0, keepdims=True)
        keep.append(jnp.broadcast_to(line, (TILE, 2 * PW)))
    keep = jnp.concatenate(keep, axis=0)

    def taps(s):
        lines = k3[s].astype(F32)
        if s == 0:
            lines = lines * (me_f > 0).astype(F32)
        if s == 2:
            lines = lines * (me_f < fields - 1).astype(F32)
        kf[s, 0:24, 256:768] = pltpu.roll(lines[0:24], 1, 1)
        kf[s, 24:48, 0:512] = lines[24:48]

    def bands(q, s):
        for t in range(2):
            p = 2 * s + t
            j0, jw = SPAN[p]
            for r in range(ranks):
                at = (t * colours + q) * ranks + r
                off = 256 + 128 * (3 - p)
                line = jnp.broadcast_to(kf[s, at : at + 1, off + j0 : off + j0 + 128 + jw], (PW, 128 + jw))
                tilted = pltpu.roll(line, 0, 1, stride=1, stride_axis=0)
                tb[q, p, :, r * jw : (r + 1) * jw] = tilted[:, 128:].astype(BF)
                line = jnp.broadcast_to(kf[s, 24 + at : 25 + at, 0:640], (TILE, 640))
                tilted = pltpu.roll(line, 0, 1, stride=1, stride_axis=0)
                at = (p * ranks + r) * TILE
                cb[q, at : at + TILE, :] = tilted.astype(BF)

    def image(q, s):
        at0 = 2 * s * ranks * TILE
        for u in range(2):
            passed = nn(cb[q, at0 : at0 + 128, 0:span], pat[q, u * TILE : u * TILE + span, :]).astype(BF)
            for t in range(2):
                p = 2 * s + t
                j0, jw = SPAN[p]
                for r in range(ranks):
                    at = (t * ranks + r) * TILE
                    cp[q, p, u * TILE : (u + 1) * TILE, r * jw : (r + 1) * jw] = passed[at : at + TILE, j0 : j0 + jw]
        parts = []
        for t in range(2):
            p = 2 * s + t
            wide = ranks * SPAN[p][1]
            parts.append(nt(cp[q, p, :, 0:wide], tb[q, p, :, 0:wide]))
        return jnp.concatenate(parts, axis=1)

    def side_copy(src, dst, i, send, recv):
        return pltpu.make_async_remote_copy(
            src_ref=src, dst_ref=dst(1 - i), send_sem=send(i), recv_sem=recv(1 - i),
            device_id={"field": side_f[2 * i]}, device_id_type=MESH,
        )

    def side_wait(src, dst, i, send, recv):
        pltpu.make_async_remote_copy(
            src_ref=src, dst_ref=dst(i), send_sem=send(i), recv_sem=recv(i),
            device_id={"field": side_f[2 * i]}, device_id_type=MESH,
        ).wait_recv()

    taps(1)
    for q in range(colours):
        bands(q, 1)
    loads[4].wait()
    for q in range(colours):
        own[q] = image(q, 1)
    for i, s in enumerate((0, 2)):
        side_wait(k3.at[1], lambda i: k3.at[2 * i], i, lambda i: k_s.at[i], lambda i: k_r.at[i])
        taps(s)
    loads[5].wait()

    def forward(q):
        for i, s in enumerate((0, 2)):
            bands(q, s)
            f1s[q, i] = image(q, s).astype(BF)
            copy = side_copy(f1s.at[q, i], lambda i: f1.at[q, i], i, lambda i: f1_s.at[q, i], lambda i: f1_r.at[q, i])
            copy.start()
            sends.append(copy)

    def mid_one(q):
        for i in range(2):
            side_wait(f1s.at[q, i], lambda i: f1.at[q, i], i, lambda i: f1_s.at[q, i], lambda i: f1_r.at[q, i])
        total = own[q] + f1[q, 0].astype(F32) + f1[q, 1].astype(F32)
        own[q] = total
        f2s[q] = total.astype(BF)
        for k in (2, 1, 3):
            copy = pltpu.make_async_remote_copy(
                src_ref=f2s.at[q], dst_ref=f2.at[q, banks - k],
                send_sem=f2_s.at[q, k], recv_sem=f2_r.at[q, banks - k],
                device_id={"bank": bank_at[k]}, device_id_type=MESH,
            )
            copy.start()
            sends.append(copy)

    def mid_two(q):
        total = own[q] - meas[q].astype(F32)
        for k in range(1, banks):
            pltpu.make_async_remote_copy(
                src_ref=f2s.at[q], dst_ref=f2.at[q, k], send_sem=f2_s.at[q, k], recv_sem=f2_r.at[q, k],
                device_id={"bank": bank_at[k]}, device_id_type=MESH,
            ).wait_recv()
            total = total + f2[q, k].astype(F32)
        rs[q, 1] = (keep * total).astype(BF)
        for i in range(2):
            copy = side_copy(rs.at[q, 1], lambda i: rs.at[q, 2 * i], i, lambda i: r_s.at[q, i], lambda i: r_r.at[q, i])
            copy.start()
            sends.append(copy)

    def residual_wait(q):
        for i in range(2):
            side_wait(rs.at[q, 1], lambda i: rs.at[q, 2 * i], i, lambda i: r_s.at[q, i], lambda i: r_r.at[q, i])

    turn_rows = flip(2 * TILE, TILE)
    turn_cols = flip(PW, PW)

    def backward(q, s):
        for t in range(2):
            p = 2 * s + t
            j0, jw = SPAN[p]
            wide = ranks * jw
            res = rs[q, s, :, t * PW : (t + 1) * PW]
            turned = nn(turn_rows, res).astype(BF)
            across_x = nt(turn_cols, res).astype(BF)
            back = nn(turned, tb[q, p, :, 0:wide]).astype(BF)
            for u in range(2):
                for r in range(ranks):
                    at = (p * ranks + r) * TILE
                    rb[u, at : at + TILE, j0 : j0 + jw] = back[u * TILE : (u + 1) * TILE, r * jw : (r + 1) * jw]
            for r in range(ranks):
                terms = nn(across_x, cp[q, p, :, r * jw : (r + 1) * jw])
                terms = jnp.concatenate([terms, jnp.zeros((PW, 128), F32)], axis=1)
                tilted = pltpu.roll(terms, 0, 1, stride=1, stride_axis=0)
                line = jnp.sum(tilted, axis=0, keepdims=True)
                low = 128 * (3 - p) + j0
                skip = max(0, -low)
                stop = min(128 + jw, 512 - low)
                at = t * ranks + r
                gp[q, s, at : at + 1, low + skip : low + stop] = line[:, skip:stop]
        at0 = 2 * s * ranks * TILE
        ct[at0 : at0 + 128, 0:span] = nt(rb[0, at0 : at0 + 128], pat[q, 0:span, :]) + nt(
            rb[1, at0 : at0 + 128], pat[q, TILE : TILE + span, :]
        )
        for at in range(2 * s * ranks, 2 * (s + 1) * ranks):
            tilted = pltpu.roll(ct[at * TILE : (at + 1) * TILE, :], 0, 1, stride=1, stride_axis=0)
            gc[at : at + 1, :] = jnp.sum(tilted, axis=0, keepdims=True)
        lines = pltpu.roll(gc[8 * s : 8 * s + 8], 640 - (TILE - 1), 1)
        gp[q, s, 8:16, :] = lines[:, 0:512]

    def backward_sides(q):
        residual_wait(q)
        for i in range(2):
            backward(q, 2 * i)
            copy = side_copy(gp.at[q, 2 * i], lambda i: gn.at[q, i], i, lambda i: g_s.at[q, i], lambda i: g_r.at[q, i])
            copy.start()
            sends.append(copy)

    one = [jnp.where(u, 1.0, 0.0) for u in uses_one]

    def tail_one(q):
        for i in range(2):
            side_wait(gp.at[q, 1], lambda i: gn.at[q, i], i, lambda i: g_s.at[q, i], lambda i: g_r.at[q, i])
        total = gp[q, 1] + gn[q, 0] + gn[q, 1]
        for kind in range(2):
            a = total[8 * kind : 8 * kind + 4]
            b = total[8 * kind + 4 : 8 * kind + 8]
            ga[q, me_c, 8 * kind : 8 * kind + 4] = a * (1.0 - one[0]) + b * (1.0 - one[1])
            ga[q, me_c, 8 * kind + 4 : 8 * kind + 8] = a * one[0] + b * one[1]
        for k in range(1, caps):
            copy = pltpu.make_async_remote_copy(
                src_ref=ga.at[q, me_c], dst_ref=ga.at[q, me_c], send_sem=c_s.at[q, k], recv_sem=c_r.at[q, caps - k],
                device_id={"cap": cap_at[k]}, device_id_type=MESH,
            )
            copy.start()
            sends.append(copy)

    def tail_two(q):
        for k in range(1, caps):
            pltpu.make_async_remote_copy(
                src_ref=ga.at[q, me_c], dst_ref=ga.at[q, cap_at[k]], send_sem=c_s.at[q, k], recv_sem=c_r.at[q, k],
                device_id={"cap": cap_at[k]}, device_id_type=MESH,
            ).wait_recv()
        total = ga[q, 0]
        for c in range(1, caps):
            total = total + ga[q, c]
        total = total * (1.0 / 32)
        for k in range(2):
            out_row[k, q] = total[4 * k : 4 * k + 4, 0:511]
            out_col[k, q] = total[8 + 4 * k : 12 + 4 * k, 0:511]

    forward(0)
    forward(1)
    forward(2)
    mid_one(0)
    mid_one(1)
    mid_one(2)
    mid_two(0)
    backward(0, 1)
    mid_two(1)
    backward(1, 1)
    mid_two(2)
    backward(2, 1)
    backward_sides(0)
    backward_sides(1)
    backward_sides(2)
    tail_one(0)
    tail_one(1)
    tail_one(2)
    tail_two(0)
    tail_two(1)
    tail_two(2)
    for copy in sends:
        copy.wait_send()


def body(pattern, measured, row_kernels, col_kernels, tile_patch, sat_tiles):
    fields, banks, caps = (lax.axis_size(a) for a in ("field", "bank", "cap"))
    _, colours, rows_ext, strip = pattern.shape
    across = fields * strip // TILE
    vm = pl.BlockSpec(memory_space=pltpu.VMEM)
    hbm = pl.BlockSpec(memory_space=pltpu.HBM)
    dma = pltpu.SemaphoreType.DMA
    out = jax.ShapeDtypeStruct(row_kernels.shape, F32)
    return pl.pallas_call(
        functools.partial(kernel, fields, banks, caps, across),
        out_shape=(out, out),
        in_specs=[hbm] * 6,
        out_specs=(vm, vm),
        scratch_shapes=[
            pltpu.SMEM(tile_patch.shape, jnp.int32),
            pltpu.VMEM(sat_tiles.shape, jnp.int32),
            pltpu.VMEM(measured.shape[1:], BF),
            pltpu.VMEM(row_kernels.shape, BF),
            pltpu.VMEM(col_kernels.shape, BF),
            pltpu.VMEM((colours, rows_ext, strip), BF),
            pltpu.VMEM((3, 48, 512), BF),
            pltpu.VMEM((3, 48, 1024), F32),
            pltpu.VMEM((colours, 6, PW, 1024), BF),
            pltpu.VMEM((colours, 384, 640), BF),
            pltpu.VMEM((colours, 6, 32, 1024), BF),
            pltpu.VMEM((colours, 32, strip), F32),
            pltpu.VMEM((colours, 2, 32, strip), BF),
            pltpu.VMEM((colours, 2, 32, strip), BF),
            pltpu.VMEM((colours, 32, strip), BF),
            pltpu.VMEM((colours, 4, 32, strip), BF),
            pltpu.VMEM((colours, 3, 32, strip), BF),
            pltpu.VMEM((2, 384, strip), BF),
            pltpu.VMEM((384, 640), F32),
            pltpu.VMEM((24, 640), F32),
            pltpu.VMEM((colours, 3, 16, 512), F32),
            pltpu.VMEM((colours, 2, 16, 512), F32),
            pltpu.VMEM((colours, caps, 16, 512), F32),
            dma((6,)), dma((2,)), dma((2,)), dma((colours, 2)), dma((colours, 2)),
            dma((colours, banks)), dma((colours, banks)), dma((colours, 2)), dma((colours, 2)),
            dma((colours, 2)), dma((colours, 2)), dma((colours, caps)), dma((colours, caps)),
        ],
        compiler_params=pltpu.CompilerParams(
            collective_id=0, has_side_effects=True, vmem_limit_bytes=62 << 20
        ),
    )(tile_patch, sat_tiles, measured, row_kernels, col_kernels, pattern)


def solution(mesh):
    return jax.shard_map(
        body,
        mesh=mesh,
        in_specs=(
            P("cap", None, None, "field"),
            P("cap", None, None, "field"),
            P("field", None, "bank", None),
            P("field", None, "bank", None),
            P("field"),
            P("cap", None),
        ),
        out_specs=(P("field", None, "bank", None), P("field", None, "bank", None)),
        check_vma=False,
    )
```

```python
import functools

import jax
import jax.numpy as jnp
from jax import lax
from jax.experimental import pallas as pl
from jax.experimental.pallas import tpu as pltpu
from jax.sharding import PartitionSpec as P

TILE = 16
PW = 128
BF = jnp.bfloat16
F32 = jnp.float32
MESH = pl.DeviceIdType.MESH

SPAN = ((0, 128), (0, 256), (0, 256), (0, 256), (0, 256), (128, 128))
FIRST = (0, 256, 128)
PACK = {0: (0, 128), 1: (128, 256), 4: (0, 256), 5: (256, 128)}


def nt(a, b):
    return lax.dot_general(a, b, (((1,), (1,)), ((), ())), preferred_element_type=F32)


def nn(a, b):
    return jnp.dot(a, b, preferred_element_type=F32)


def flip(rows, block):
    i = lax.broadcasted_iota(jnp.int32, (rows, rows), 0)
    j = lax.broadcasted_iota(jnp.int32, (rows, rows), 1)
    same = (i // block) == (j // block)
    return (same & ((i % block) + (j % block) == block - 1)).astype(F32).astype(BF)


def kernel(
    fields, banks, caps, across,
    tile_hbm, sat_hbm, meas_hbm, rowk_hbm, colk_hbm, pat_hbm,
    out_row, out_col,
    tile_ref, sat, meas, rowk, colk, pat,
    k3, kf, tb, cb, cp, own, f1s, f1, f2s, f2, rs, rb, ct, gc, gp, gq, gs, gn, ga,
    in_sem, k_s, k_r, f1_s, f1_r, f2_s, f2_r, r_s, r_r, g_s, g_r, c_s, c_r, seen,
):
    colours, ranks = 3, 4
    rows_ext = pat.shape[1]
    span = rows_ext - TILE
    me_f = lax.axis_index("field")
    me_b = lax.axis_index("bank")
    me_c = lax.axis_index("cap")
    side_f = (lax.rem(me_f + fields - 1, fields), me_f, lax.rem(me_f + 1, fields))
    bank_at = [lax.rem(me_b + k, banks) for k in range(banks)]
    cap_at = [lax.rem(me_c + k, caps) for k in range(caps)]

    barrier = pltpu.get_barrier_semaphore()
    for k in (1, banks - 1):
        pl.semaphore_signal(barrier, inc=1, device_id={"bank": bank_at[k]}, device_id_type=MESH)
    for s in (0, 2):
        pl.semaphore_signal(barrier, inc=1, device_id={"field": side_f[s]}, device_id_type=MESH)
    for k in range(1, caps):
        pl.semaphore_signal(barrier, inc=1, device_id={"cap": cap_at[k]}, device_id_type=MESH)

    loads = [
        pltpu.make_async_copy(src, dst, in_sem.at[i])
        for i, (src, dst) in enumerate(
            ((tile_hbm, tile_ref), (rowk_hbm, rowk), (colk_hbm, colk), (sat_hbm, sat), (pat_hbm.at[0], pat), (meas_hbm.at[0], meas))
        )
    ]
    for load in loads:
        load.start()

    rb[...] = jnp.zeros(rb.shape, BF)
    ct[...] = jnp.zeros(ct.shape, F32)
    k3[1] = jnp.zeros((48, 512), BF)
    kf[...] = jnp.zeros(kf.shape, F32)

    for load in loads[0:4]:
        load.wait()
    uses_one = [tile_ref[t] == 1 for t in range(2)]
    for kind, ref in ((0, rowk), (1, colk)):
        for t in range(2):
            for q in range(colours):
                at = ((kind * 2 + t) * colours + q) * ranks
                first = ref[0, q].astype(F32)
                second = ref[1, q].astype(F32)
                k3[1, at : at + ranks, 0:511] = jnp.where(uses_one[t], second, first).astype(BF)

    pl.semaphore_wait(barrier, 2 + 2 + caps - 1)
    sends = []
    for i, s in enumerate((0, 2)):
        copy = pltpu.make_async_remote_copy(
            src_ref=k3.at[1], dst_ref=k3.at[2 - s], send_sem=k_s.at[i], recv_sem=k_r.at[1 - i],
            device_id={"field": side_f[s]}, device_id_type=MESH,
        )
        copy.start()
        sends.append(copy)
    pl.semaphore_signal(seen, inc=1, device_id={"bank": bank_at[banks - 1]}, device_id_type=MESH)

    tiles = 2 * PW // TILE
    sub = lax.broadcasted_iota(jnp.int32, (tiles, sat.shape[1]), 0)
    listed = jnp.broadcast_to(sat[0:1, :], (tiles, sat.shape[1]))
    lane_tile = lax.broadcasted_iota(jnp.int32, (tiles, 2 * PW), 1) // TILE
    mine = (lane_tile == lax.broadcasted_iota(jnp.int32, (tiles, 2 * PW), 0)).astype(F32)
    keep = []
    for h in range(2):
        hit = (listed == sub + (h * across + me_f * tiles)).astype(F32)
        hit = jnp.max(hit, axis=1, keepdims=True)
        line = 1.0 - jnp.sum(hit * mine, axis=0, keepdims=True)
        keep.append(jnp.broadcast_to(line, (TILE, 2 * PW)))
    keep = jnp.concatenate(keep, axis=0)

    def taps(s):
        lines = k3[s].astype(F32)
        if s == 0:
            lines = lines * (me_f > 0).astype(F32)
        if s == 2:
            lines = lines * (me_f < fields - 1).astype(F32)
        kf[s, 0:24, 256:768] = pltpu.roll(lines[0:24], 1, 1)
        kf[s, 24:48, 0:512] = lines[24:48]

    def bands(q, s):
        for t in range(2):
            p = 2 * s + t
            j0, jw = SPAN[p]
            for r in range(ranks):
                at = (t * colours + q) * ranks + r
                off = 256 + 128 * (3 - p)
                line = jnp.broadcast_to(kf[s, at : at + 1, off + j0 : off + j0 + 128 + jw], (PW, 128 + jw))
                tilted = pltpu.roll(line, 0, 1, stride=1, stride_axis=0)
                tb[q, p, :, r * jw : (r + 1) * jw] = tilted[:, 128:].astype(BF)
                line = jnp.broadcast_to(kf[s, 24 + at : 25 + at, 0:640], (TILE, 640))
                tilted = pltpu.roll(line, 0, 1, stride=1, stride_axis=0)
                at = FIRST[s] + (t * ranks + r) * TILE
                cb[q, at : at + TILE, :] = tilted.astype(BF)

    def columns(q, strips):
        at0 = FIRST[strips[0]]
        count = len(strips) * 2 * ranks * TILE
        for u in range(2):
            passed = nn(cb[q, at0 : at0 + count, 0:span], pat[q, u * TILE : u * TILE + span, :]).astype(BF)
            for s in strips:
                for t in range(2):
                    p = 2 * s + t
                    j0, jw = SPAN[p]
                    for r in range(ranks):
                        at = FIRST[s] - at0 + (t * ranks + r) * TILE
                        cp[q, p, u * TILE : (u + 1) * TILE, r * jw : (r + 1) * jw] = passed[at : at + TILE, j0 : j0 + jw]

    def image(q, s):
        parts = []
        for t in range(2):
            p = 2 * s + t
            wide = ranks * SPAN[p][1]
            parts.append(nt(cp[q, p, :, 0:wide], tb[q, p, :, 0:wide]))
        return jnp.concatenate(parts, axis=1)

    def side_copy(src, dst, i, send, recv):
        return pltpu.make_async_remote_copy(
            src_ref=src, dst_ref=dst(1 - i), send_sem=send(i), recv_sem=recv(1 - i),
            device_id={"field": side_f[2 * i]}, device_id_type=MESH,
        )

    def side_wait(src, dst, i, send, recv):
        pltpu.make_async_remote_copy(
            src_ref=src, dst_ref=dst(i), send_sem=send(i), recv_sem=recv(i),
            device_id={"field": side_f[2 * i]}, device_id_type=MESH,
        ).wait_recv()

    taps(1)
    for q in range(colours):
        bands(q, 1)
    loads[4].wait()
    for q in range(colours):
        columns(q, (1,))
        own[q] = image(q, 1)
    for i, s in enumerate((0, 2)):
        side_wait(k3.at[1], lambda i: k3.at[2 * i], i, lambda i: k_s.at[i], lambda i: k_r.at[i])
        taps(s)
    loads[5].wait()
    pl.semaphore_wait(seen, 1)

    def forward(q):
        for s in (0, 2):
            bands(q, s)
        columns(q, (0, 2))
        for i, s in enumerate((0, 2)):
            f1s[q, i] = image(q, s).astype(BF)
            copy = side_copy(f1s.at[q, i], lambda i: f1.at[q, i], i, lambda i: f1_s.at[q, i], lambda i: f1_r.at[q, i])
            copy.start()
            sends.append(copy)

    def mid_one(q):
        for i in range(2):
            side_wait(f1s.at[q, i], lambda i: f1.at[q, i], i, lambda i: f1_s.at[q, i], lambda i: f1_r.at[q, i])
        total = own[q] + f1[q, 0].astype(F32) + f1[q, 1].astype(F32)
        own[q] = total
        f2s[q] = total.astype(BF)
        for k in (2, 1, 3):
            copy = pltpu.make_async_remote_copy(
                src_ref=f2s.at[q], dst_ref=f2.at[q, banks - k],
                send_sem=f2_s.at[q, k], recv_sem=f2_r.at[q, banks - k],
                device_id={"bank": bank_at[k]}, device_id_type=MESH,
            )
            copy.start()
            sends.append(copy)

    def mid_two(q):
        total = own[q] - meas[q].astype(F32)
        for k in range(1, banks):
            pltpu.make_async_remote_copy(
                src_ref=f2s.at[q], dst_ref=f2.at[q, k], send_sem=f2_s.at[q, k], recv_sem=f2_r.at[q, k],
                device_id={"bank": bank_at[k]}, device_id_type=MESH,
            ).wait_recv()
            total = total + f2[q, k].astype(F32)
        rs[q, 1] = (keep * total).astype(BF)
        for i in range(2):
            copy = side_copy(rs.at[q, 1], lambda i: rs.at[q, 2 * i], i, lambda i: r_s.at[q, i], lambda i: r_r.at[q, i])
            copy.start()
            sends.append(copy)

    def residual_wait(q):
        for i in range(2):
            side_wait(rs.at[q, 1], lambda i: rs.at[q, 2 * i], i, lambda i: r_s.at[q, i], lambda i: r_r.at[q, i])

    turn_rows = flip(2 * TILE, TILE)
    turn_cols = flip(PW, PW)

    def backward(q, strips):
        for s in strips:
            turned = nn(turn_rows, rs[q, s]).astype(BF)
            for t in range(2):
                p = 2 * s + t
                j0, jw = SPAN[p]
                wide = ranks * jw
                across_x = nt(turn_cols, rs[q, s, :, t * PW : (t + 1) * PW]).astype(BF)
                back = nn(turned[:, t * PW : (t + 1) * PW], tb[q, p, :, 0:wide]).astype(BF)
                for u in range(2):
                    for r in range(ranks):
                        at = FIRST[s] + (t * ranks + r) * TILE
                        rb[u, at : at + TILE, j0 : j0 + jw] = back[u * TILE : (u + 1) * TILE, r * jw : (r + 1) * jw]
                for r in range(ranks):
                    terms = nn(across_x, cp[q, p, :, r * jw : (r + 1) * jw])
                    terms = jnp.concatenate([terms, jnp.zeros((PW, 128), F32)], axis=1)
                    tilted = pltpu.roll(terms, 0, 1, stride=1, stride_axis=0)
                    line = jnp.sum(tilted, axis=0, keepdims=True)
                    low = 128 * (3 - p) + j0
                    skip = max(0, -low)
                    stop = min(128 + jw, 512 - low)
                    at = t * ranks + r
                    if s == 1:
                        both = [line[:, 0:384], jnp.zeros((1, 128), F32)]
                        gp[at : at + 1, :] = jnp.concatenate(both if t else both[::-1], axis=1)
                    else:
                        off, wide_off = PACK[p]
                        gq[s // 2, r : r + 1, off : off + wide_off] = line[:, skip:stop]
        at0 = FIRST[strips[0]]
        at1 = at0 + len(strips) * 2 * ranks * TILE
        ct[at0:at1, 0:span] = nt(rb[0, at0:at1], pat[q, 0:span, :]) + nt(rb[1, at0:at1], pat[q, TILE : TILE + span, :])
        for at in range(at0 // TILE, at1 // TILE):
            tilted = pltpu.roll(ct[at * TILE : (at + 1) * TILE, :], 0, 1, stride=1, stride_axis=0)
            gc[at : at + 1, :] = jnp.sum(tilted, axis=0, keepdims=True)
        for s in strips:
            at = FIRST[s] // TILE
            lines = pltpu.roll(gc[at : at + 8], 640 - (TILE - 1), 1)
            if s == 1:
                gp[8:16, :] = lines[:, 0:512]
            else:
                last = [lines[0:4, 384:512], lines[4:8, 384:512], jnp.zeros((4, 128), F32)]
                low = jnp.concatenate([gq[s // 2], jnp.concatenate(last, axis=1)], axis=0)
                gs[q, s // 2] = jnp.concatenate([lines[:, 0:384], low], axis=0).astype(BF)

    def unpack(m, i):
        ends = jnp.concatenate([m[12:16, 0:128], m[12:16, 128:256]], axis=0)
        cols = jnp.concatenate([m[0:8], ends], axis=1)
        parts = []
        for t in range(2):
            p = 4 * (1 - i) + t
            off, wide = PACK[p]
            piece = [m[8:12, off : off + wide], jnp.zeros((4, 512 - wide), F32)]
            parts.append(jnp.concatenate(piece[::-1] if i == 1 else piece, axis=1))
        return jnp.concatenate([*parts, cols], axis=0)

    def backward_own(q):
        backward(q, (1,))
        ga[q, me_c] = gp[...]
        for k in range(1, caps):
            copy = pltpu.make_async_remote_copy(
                src_ref=ga.at[q, me_c], dst_ref=ga.at[q, me_c], send_sem=c_s.at[q, k], recv_sem=c_r.at[q, caps - k],
                device_id={"cap": cap_at[k]}, device_id_type=MESH,
            )
            copy.start()
            sends.append(copy)

    def backward_sides(q):
        residual_wait(q)
        backward(q, (0, 2))
        for i in range(2):
            for k in range(caps):
                copy = pltpu.make_async_remote_copy(
                    src_ref=gs.at[q, i], dst_ref=gn.at[q, 1 - i, me_c],
                    send_sem=g_s.at[q, i, k], recv_sem=g_r.at[q, 1 - i, (caps - k) % caps],
                    device_id={"field": side_f[2 * i], "cap": cap_at[k]}, device_id_type=MESH,
                )
                copy.start()
                sends.append(copy)

    one = [jnp.where(u, 1.0, 0.0) for u in uses_one]

    def tail(q):
        for k in range(1, caps):
            pltpu.make_async_remote_copy(
                src_ref=ga.at[q, me_c], dst_ref=ga.at[q, cap_at[k]], send_sem=c_s.at[q, k], recv_sem=c_r.at[q, k],
                device_id={"cap": cap_at[k]}, device_id_type=MESH,
            ).wait_recv()
        for i in range(2):
            for k in range(caps):
                pltpu.make_async_remote_copy(
                    src_ref=gs.at[q, i], dst_ref=gn.at[q, i, cap_at[k]], send_sem=g_s.at[q, i, k], recv_sem=g_r.at[q, i, k],
                    device_id={"field": side_f[2 * i], "cap": cap_at[k]}, device_id_type=MESH,
                ).wait_recv()
        total = ga[q, 0]
        for c in range(1, caps):
            total = total + ga[q, c]
        for i in range(2):
            side = gn[q, i, 0].astype(F32)
            for c in range(1, caps):
                side = side + gn[q, i, c].astype(F32)
            total = total + unpack(side, i)
        total = total * (1.0 / 32)
        for kind, out in ((0, out_row), (1, out_col)):
            a = total[8 * kind : 8 * kind + 4, 0:511]
            b = total[8 * kind + 4 : 8 * kind + 8, 0:511]
            out[0, q] = a * (1.0 - one[0]) + b * (1.0 - one[1])
            out[1, q] = a * one[0] + b * one[1]

    forward(0)
    forward(1)
    forward(2)
    mid_one(0)
    mid_one(1)
    mid_one(2)
    mid_two(0)
    backward_own(0)
    mid_two(1)
    backward_own(1)
    mid_two(2)
    backward_own(2)
    backward_sides(0)
    backward_sides(1)
    backward_sides(2)
    tail(0)
    tail(1)
    tail(2)
    for copy in sends:
        copy.wait_send()


def body(pattern, measured, row_kernels, col_kernels, tile_patch, sat_tiles):
    fields, banks, caps = (lax.axis_size(a) for a in ("field", "bank", "cap"))
    _, colours, rows_ext, strip = pattern.shape
    across = fields * strip // TILE
    vm = pl.BlockSpec(memory_space=pltpu.VMEM)
    hbm = pl.BlockSpec(memory_space=pltpu.HBM)
    dma = pltpu.SemaphoreType.DMA
    out = jax.ShapeDtypeStruct(row_kernels.shape, F32)
    return pl.pallas_call(
        functools.partial(kernel, fields, banks, caps, across),
        out_shape=(out, out),
        in_specs=[hbm] * 6,
        out_specs=(vm, vm),
        scratch_shapes=[
            pltpu.SMEM(tile_patch.shape, jnp.int32),
            pltpu.VMEM(sat_tiles.shape, jnp.int32),
            pltpu.VMEM(measured.shape[1:], BF),
            pltpu.VMEM(row_kernels.shape, BF),
            pltpu.VMEM(col_kernels.shape, BF),
            pltpu.VMEM((colours, rows_ext, strip), BF),
            pltpu.VMEM((3, 48, 512), BF),
            pltpu.VMEM((3, 48, 1024), F32),
            pltpu.VMEM((colours, 6, PW, 1024), BF),
            pltpu.VMEM((colours, 384, 640), BF),
            pltpu.VMEM((colours, 6, 32, 1024), BF),
            pltpu.VMEM((colours, 32, strip), F32),
            pltpu.VMEM((colours, 2, 32, strip), BF),
            pltpu.VMEM((colours, 2, 32, strip), BF),
            pltpu.VMEM((colours, 32, strip), BF),
            pltpu.VMEM((colours, 4, 32, strip), BF),
            pltpu.VMEM((colours, 3, 32, strip), BF),
            pltpu.VMEM((2, 384, strip), BF),
            pltpu.VMEM((384, 640), F32),
            pltpu.VMEM((24, 640), F32),
            pltpu.VMEM((16, 512), F32),
            pltpu.VMEM((2, 4, 384), F32),
            pltpu.VMEM((colours, 2, 16, 384), BF),
            pltpu.VMEM((colours, 2, caps, 16, 384), BF),
            pltpu.VMEM((colours, caps, 16, 512), F32),
            dma((6,)), dma((2,)), dma((2,)), dma((colours, 2)), dma((colours, 2)),
            dma((colours, banks)), dma((colours, banks)), dma((colours, 2)), dma((colours, 2)),
            dma((colours, 2, caps)), dma((colours, 2, caps)), dma((colours, caps)), dma((colours, caps)),
            pltpu.SemaphoreType.REGULAR,
        ],
        compiler_params=pltpu.CompilerParams(
            collective_id=0, has_side_effects=True, vmem_limit_bytes=62 << 20
        ),
    )(tile_patch, sat_tiles, measured, row_kernels, col_kernels, pattern)


def solution(mesh):
    return jax.shard_map(
        body,
        mesh=mesh,
        in_specs=(
            P("cap", None, None, "field"),
            P("cap", None, None, "field"),
            P("field", None, "bank", None),
            P("field", None, "bank", None),
            P("field"),
            P("cap", None),
        ),
        out_specs=(P("field", None, "bank", None), P("field", None, "bank", None)),
        check_vma=False,
    )
```

```python
import functools

import jax
import jax.numpy as jnp
from jax import lax
from jax.experimental import pallas as pl
from jax.experimental.pallas import tpu as pltpu
from jax.sharding import PartitionSpec as P

TILE = 16
PW = 128
BF = jnp.bfloat16
F32 = jnp.float32
MESH = pl.DeviceIdType.MESH

SPAN = ((0, 128), (0, 256), (0, 256), (0, 256), (0, 256), (128, 128))
FIRST = (0, 256, 128)
PACK = {0: (0, 128), 1: (128, 256), 4: (0, 256), 5: (256, 128)}


def nt(a, b):
    return lax.dot_general(a, b, (((1,), (1,)), ((), ())), preferred_element_type=F32)


def nn(a, b):
    return jnp.dot(a, b, preferred_element_type=F32)


def flip(rows, block):
    i = lax.broadcasted_iota(jnp.int32, (rows, rows), 0)
    j = lax.broadcasted_iota(jnp.int32, (rows, rows), 1)
    same = (i // block) == (j // block)
    return (same & ((i % block) + (j % block) == block - 1)).astype(F32).astype(BF)


def kernel(
    fields, banks, caps, across,
    tile_hbm, sat_hbm, meas_hbm, rowk_hbm, colk_hbm, pat_hbm,
    out_row, out_col,
    tile_ref, sat, meas, rowk, colk, pat,
    k3, kf, tb, cb, cp, own, f1s, f1, f2s, f2, rs, rb, ct, gc, gp, gq, gs, gn, ga,
    in_sem, k_s, k_r, f1_s, f1_r, f2_s, f2_r, r_s, r_r, g_s, g_r, c_s, c_r, seen,
):
    colours, ranks = 3, 4
    rows_ext = pat.shape[1]
    span = rows_ext - TILE
    me_f = lax.axis_index("field")
    me_b = lax.axis_index("bank")
    me_c = lax.axis_index("cap")
    side_f = (lax.rem(me_f + fields - 1, fields), me_f, lax.rem(me_f + 1, fields))
    bank_at = [lax.rem(me_b + k, banks) for k in range(banks)]
    cap_at = [lax.rem(me_c + k, caps) for k in range(caps)]

    has = (me_f > 0, me_f < fields - 1)
    ends = ((me_f == 0).astype(jnp.int32), (me_f == fields - 1).astype(jnp.int32))

    barrier = pltpu.get_barrier_semaphore()
    for k in (1, banks - 1):
        pl.semaphore_signal(barrier, inc=1, device_id={"bank": bank_at[k]}, device_id_type=MESH)
    for i in range(2):

        @pl.when(has[i])
        def _(i=i):
            pl.semaphore_signal(barrier, inc=1, device_id={"field": side_f[2 * i]}, device_id_type=MESH)

        @pl.when(jnp.logical_not(has[i]))
        def _(i=i):
            k3[2 * i] = jnp.zeros((48, 512), BF)
            for q in range(colours):
                f1[q, i] = jnp.zeros(f1.shape[2:], BF)
                rs[q, 2 * i] = jnp.zeros(rs.shape[2:], BF)
                gn[q, i] = jnp.zeros(gn.shape[2:], BF)

    for k in range(1, caps):
        pl.semaphore_signal(barrier, inc=1, device_id={"cap": cap_at[k]}, device_id_type=MESH)

    loads = [
        pltpu.make_async_copy(src, dst, in_sem.at[i])
        for i, (src, dst) in enumerate(
            ((tile_hbm, tile_ref), (rowk_hbm, rowk), (colk_hbm, colk), (sat_hbm, sat), (pat_hbm.at[0], pat), (meas_hbm.at[0], meas))
        )
    ]
    for load in loads:
        load.start()

    rb[...] = jnp.zeros(rb.shape, BF)
    ct[...] = jnp.zeros(ct.shape, F32)
    k3[1] = jnp.zeros((48, 512), BF)
    kf[...] = jnp.zeros(kf.shape, F32)

    for load in loads[0:4]:
        load.wait()
    uses_one = [tile_ref[t] == 1 for t in range(2)]
    for kind, ref in ((0, rowk), (1, colk)):
        for t in range(2):
            for q in range(colours):
                at = ((kind * 2 + t) * colours + q) * ranks
                first = ref[0, q].astype(F32)
                second = ref[1, q].astype(F32)
                k3[1, at : at + ranks, 0:511] = jnp.where(uses_one[t], second, first).astype(BF)

    pl.semaphore_wait(barrier, 2 + 2 + caps - 1 - ends[0] - ends[1])
    sends = []

    def to_side(copies, i):
        @pl.when(has[i])
        def _():
            for copy in copies:
                copy.start()

        sends.append((i, copies))

    for i, s in enumerate((0, 2)):
        copy = pltpu.make_async_remote_copy(
            src_ref=k3.at[1], dst_ref=k3.at[2 - s], send_sem=k_s.at[i], recv_sem=k_r.at[1 - i],
            device_id={"field": side_f[s]}, device_id_type=MESH,
        )
        to_side([copy], i)
    pl.semaphore_signal(seen, inc=1, device_id={"bank": bank_at[banks - 1]}, device_id_type=MESH)

    tiles = 2 * PW // TILE
    sub = lax.broadcasted_iota(jnp.int32, (tiles, sat.shape[1]), 0)
    listed = jnp.broadcast_to(sat[0:1, :], (tiles, sat.shape[1]))
    lane_tile = lax.broadcasted_iota(jnp.int32, (tiles, 2 * PW), 1) // TILE
    mine = (lane_tile == lax.broadcasted_iota(jnp.int32, (tiles, 2 * PW), 0)).astype(F32)
    keep = []
    for h in range(2):
        hit = (listed == sub + (h * across + me_f * tiles)).astype(F32)
        hit = jnp.max(hit, axis=1, keepdims=True)
        line = 1.0 - jnp.sum(hit * mine, axis=0, keepdims=True)
        keep.append(jnp.broadcast_to(line, (TILE, 2 * PW)))
    keep = jnp.concatenate(keep, axis=0)

    def taps(s):
        lines = k3[s].astype(F32)
        kf[s, 0:24, 256:768] = pltpu.roll(lines[0:24], 1, 1)
        kf[s, 24:48, 0:512] = lines[24:48]

    def bands(q, s):
        for t in range(2):
            p = 2 * s + t
            j0, jw = SPAN[p]
            for r in range(ranks):
                at = (t * colours + q) * ranks + r
                off = 256 + 128 * (3 - p)
                line = jnp.broadcast_to(kf[s, at : at + 1, off + j0 : off + j0 + 128 + jw], (PW, 128 + jw))
                tilted = pltpu.roll(line, 0, 1, stride=1, stride_axis=0)
                tb[q, p, :, r * jw : (r + 1) * jw] = tilted[:, 128:].astype(BF)
                line = jnp.broadcast_to(kf[s, 24 + at : 25 + at, 0:640], (TILE, 640))
                tilted = pltpu.roll(line, 0, 1, stride=1, stride_axis=0)
                at = FIRST[s] + (t * ranks + r) * TILE
                cb[q, at : at + TILE, :] = tilted.astype(BF)

    def columns(q, strips):
        at0 = FIRST[strips[0]]
        count = len(strips) * 2 * ranks * TILE
        for u in range(2):
            passed = nn(cb[q, at0 : at0 + count, 0:span], pat[q, u * TILE : u * TILE + span, :]).astype(BF)
            for s in strips:
                for t in range(2):
                    p = 2 * s + t
                    j0, jw = SPAN[p]
                    for r in range(ranks):
                        at = FIRST[s] - at0 + (t * ranks + r) * TILE
                        cp[q, p, u * TILE : (u + 1) * TILE, r * jw : (r + 1) * jw] = passed[at : at + TILE, j0 : j0 + jw]

    def image(q, s):
        parts = []
        for t in range(2):
            p = 2 * s + t
            wide = ranks * SPAN[p][1]
            parts.append(nt(cp[q, p, :, 0:wide], tb[q, p, :, 0:wide]))
        return jnp.concatenate(parts, axis=1)

    def side_copy(src, dst, i, send, recv):
        return pltpu.make_async_remote_copy(
            src_ref=src, dst_ref=dst(1 - i), send_sem=send(i), recv_sem=recv(1 - i),
            device_id={"field": side_f[2 * i]}, device_id_type=MESH,
        )

    def side_wait(src, dst, i, send, recv):
        @pl.when(has[i])
        def _():
            pltpu.make_async_remote_copy(
                src_ref=src, dst_ref=dst(i), send_sem=send(i), recv_sem=recv(i),
                device_id={"field": side_f[2 * i]}, device_id_type=MESH,
            ).wait_recv()

    taps(1)
    for q in range(colours):
        bands(q, 1)
    loads[4].wait()
    for q in range(colours):
        columns(q, (1,))
        own[q] = image(q, 1)
    for i, s in enumerate((0, 2)):
        side_wait(k3.at[1], lambda i: k3.at[2 * i], i, lambda i: k_s.at[i], lambda i: k_r.at[i])
        taps(s)
    loads[5].wait()
    pl.semaphore_wait(seen, 1)

    def forward(q):
        for s in (0, 2):
            bands(q, s)
        columns(q, (0, 2))
        for i, s in enumerate((0, 2)):
            f1s[q, i] = image(q, s).astype(BF)
            copy = side_copy(f1s.at[q, i], lambda i: f1.at[q, i], i, lambda i: f1_s.at[q, i], lambda i: f1_r.at[q, i])
            to_side([copy], i)

    def mid_one(q):
        for i in range(2):
            side_wait(f1s.at[q, i], lambda i: f1.at[q, i], i, lambda i: f1_s.at[q, i], lambda i: f1_r.at[q, i])
        total = own[q] + f1[q, 0].astype(F32) + f1[q, 1].astype(F32)
        own[q] = total
        f2s[q] = total.astype(BF)
        for k in (2, 1, 3):
            copy = pltpu.make_async_remote_copy(
                src_ref=f2s.at[q], dst_ref=f2.at[q, banks - k],
                send_sem=f2_s.at[q, k], recv_sem=f2_r.at[q, banks - k],
                device_id={"bank": bank_at[k]}, device_id_type=MESH,
            )
            copy.start()
            sends.append((2, [copy]))

    def mid_two(q):
        total = own[q] - meas[q].astype(F32)
        for k in range(1, banks):
            pltpu.make_async_remote_copy(
                src_ref=f2s.at[q], dst_ref=f2.at[q, k], send_sem=f2_s.at[q, k], recv_sem=f2_r.at[q, k],
                device_id={"bank": bank_at[k]}, device_id_type=MESH,
            ).wait_recv()
            total = total + f2[q, k].astype(F32)
        rs[q, 1] = (keep * total).astype(BF)
        for i in range(2):
            copy = side_copy(rs.at[q, 1], lambda i: rs.at[q, 2 * i], i, lambda i: r_s.at[q, i], lambda i: r_r.at[q, i])
            to_side([copy], i)

    def residual_wait(q):
        for i in range(2):
            side_wait(rs.at[q, 1], lambda i: rs.at[q, 2 * i], i, lambda i: r_s.at[q, i], lambda i: r_r.at[q, i])

    turn_rows = flip(2 * TILE, TILE)
    turn_cols = flip(PW, PW)

    def backward(q, strips):
        for s in strips:
            turned = nn(turn_rows, rs[q, s]).astype(BF)
            for t in range(2):
                p = 2 * s + t
                j0, jw = SPAN[p]
                wide = ranks * jw
                across_x = nt(turn_cols, rs[q, s, :, t * PW : (t + 1) * PW]).astype(BF)
                back = nn(turned[:, t * PW : (t + 1) * PW], tb[q, p, :, 0:wide]).astype(BF)
                for u in range(2):
                    for r in range(ranks):
                        at = FIRST[s] + (t * ranks + r) * TILE
                        rb[u, at : at + TILE, j0 : j0 + jw] = back[u * TILE : (u + 1) * TILE, r * jw : (r + 1) * jw]
                for r in range(ranks):
                    terms = nn(across_x, cp[q, p, :, r * jw : (r + 1) * jw])
                    terms = jnp.concatenate([terms, jnp.zeros((PW, 128), F32)], axis=1)
                    tilted = pltpu.roll(terms, 0, 1, stride=1, stride_axis=0)
                    line = jnp.sum(tilted, axis=0, keepdims=True)
                    low = 128 * (3 - p) + j0
                    skip = max(0, -low)
                    stop = min(128 + jw, 512 - low)
                    at = t * ranks + r
                    if s == 1:
                        both = [line[:, 0:384], jnp.zeros((1, 128), F32)]
                        gp[at : at + 1, :] = jnp.concatenate(both if t else both[::-1], axis=1)
                    else:
                        off, wide_off = PACK[p]
                        gq[s // 2, r : r + 1, off : off + wide_off] = line[:, skip:stop]
        at0 = FIRST[strips[0]]
        at1 = at0 + len(strips) * 2 * ranks * TILE
        ct[at0:at1, 0:span] = nt(rb[0, at0:at1], pat[q, 0:span, :]) + nt(rb[1, at0:at1], pat[q, TILE : TILE + span, :])
        for at in range(at0 // TILE, at1 // TILE):
            tilted = pltpu.roll(ct[at * TILE : (at + 1) * TILE, :], 0, 1, stride=1, stride_axis=0)
            gc[at : at + 1, :] = jnp.sum(tilted, axis=0, keepdims=True)
        for s in strips:
            at = FIRST[s] // TILE
            lines = pltpu.roll(gc[at : at + 8], 640 - (TILE - 1), 1)
            if s == 1:
                gp[8:16, :] = lines[:, 0:512]
            else:
                last = [lines[0:4, 384:512], lines[4:8, 384:512], jnp.zeros((4, 128), F32)]
                low = jnp.concatenate([gq[s // 2], jnp.concatenate(last, axis=1)], axis=0)
                gs[q, s // 2] = jnp.concatenate([lines[:, 0:384], low], axis=0).astype(BF)

    def unpack(m, i):
        ends = jnp.concatenate([m[12:16, 0:128], m[12:16, 128:256]], axis=0)
        cols = jnp.concatenate([m[0:8], ends], axis=1)
        parts = []
        for t in range(2):
            p = 4 * (1 - i) + t
            off, wide = PACK[p]
            piece = [m[8:12, off : off + wide], jnp.zeros((4, 512 - wide), F32)]
            parts.append(jnp.concatenate(piece[::-1] if i == 1 else piece, axis=1))
        return jnp.concatenate([*parts, cols], axis=0)

    def backward_own(q):
        backward(q, (1,))
        ga[q, me_c] = gp[...]
        for k in range(1, caps):
            copy = pltpu.make_async_remote_copy(
                src_ref=ga.at[q, me_c], dst_ref=ga.at[q, me_c], send_sem=c_s.at[q, k], recv_sem=c_r.at[q, caps - k],
                device_id={"cap": cap_at[k]}, device_id_type=MESH,
            )
            copy.start()
            sends.append((2, [copy]))

    def backward_sides(q):
        residual_wait(q)
        backward(q, (0, 2))
        for i in range(2):
            copies = []
            for k in range(caps):
                copy = pltpu.make_async_remote_copy(
                    src_ref=gs.at[q, i], dst_ref=gn.at[q, 1 - i, me_c],
                    send_sem=g_s.at[q, i, k], recv_sem=g_r.at[q, 1 - i, (caps - k) % caps],
                    device_id={"field": side_f[2 * i], "cap": cap_at[k]}, device_id_type=MESH,
                )
                copies.append(copy)
            to_side(copies, i)

    one = [jnp.where(u, 1.0, 0.0) for u in uses_one]

    def tail(q):
        for k in range(1, caps):
            pltpu.make_async_remote_copy(
                src_ref=ga.at[q, me_c], dst_ref=ga.at[q, cap_at[k]], send_sem=c_s.at[q, k], recv_sem=c_r.at[q, k],
                device_id={"cap": cap_at[k]}, device_id_type=MESH,
            ).wait_recv()
        for i in range(2):

            @pl.when(has[i])
            def _(i=i):
                for k in range(caps):
                    pltpu.make_async_remote_copy(
                        src_ref=gs.at[q, i], dst_ref=gn.at[q, i, cap_at[k]],
                        send_sem=g_s.at[q, i, k], recv_sem=g_r.at[q, i, k],
                        device_id={"field": side_f[2 * i], "cap": cap_at[k]}, device_id_type=MESH,
                    ).wait_recv()

        total = ga[q, 0]
        for c in range(1, caps):
            total = total + ga[q, c]
        for i in range(2):
            side = gn[q, i, 0].astype(F32)
            for c in range(1, caps):
                side = side + gn[q, i, c].astype(F32)
            total = total + unpack(side, i)
        total = total * (1.0 / 32)
        for kind, out in ((0, out_row), (1, out_col)):
            a = total[8 * kind : 8 * kind + 4, 0:511]
            b = total[8 * kind + 4 : 8 * kind + 8, 0:511]
            out[0, q] = a * (1.0 - one[0]) + b * (1.0 - one[1])
            out[1, q] = a * one[0] + b * one[1]

    forward(0)
    forward(1)
    forward(2)
    mid_one(0)
    mid_one(1)
    mid_one(2)
    mid_two(0)
    backward_own(0)
    mid_two(1)
    backward_own(1)
    mid_two(2)
    backward_own(2)
    backward_sides(0)
    backward_sides(1)
    backward_sides(2)
    tail(0)
    tail(1)
    tail(2)
    for i in range(3):
        mine = [copy for to, copies in sends for copy in copies if to == i]
        if i == 2:
            for copy in mine:
                copy.wait_send()
        else:

            @pl.when(has[i])
            def _(mine=mine):
                for copy in mine:
                    copy.wait_send()


def body(pattern, measured, row_kernels, col_kernels, tile_patch, sat_tiles):
    fields, banks, caps = (lax.axis_size(a) for a in ("field", "bank", "cap"))
    _, colours, rows_ext, strip = pattern.shape
    across = fields * strip // TILE
    vm = pl.BlockSpec(memory_space=pltpu.VMEM)
    hbm = pl.BlockSpec(memory_space=pltpu.HBM)
    dma = pltpu.SemaphoreType.DMA
    out = jax.ShapeDtypeStruct(row_kernels.shape, F32)
    return pl.pallas_call(
        functools.partial(kernel, fields, banks, caps, across),
        out_shape=(out, out),
        in_specs=[hbm] * 6,
        out_specs=(vm, vm),
        scratch_shapes=[
            pltpu.SMEM(tile_patch.shape, jnp.int32),
            pltpu.VMEM(sat_tiles.shape, jnp.int32),
            pltpu.VMEM(measured.shape[1:], BF),
            pltpu.VMEM(row_kernels.shape, BF),
            pltpu.VMEM(col_kernels.shape, BF),
            pltpu.VMEM((colours, rows_ext, strip), BF),
            pltpu.VMEM((3, 48, 512), BF),
            pltpu.VMEM((3, 48, 1024), F32),
            pltpu.VMEM((colours, 6, PW, 1024), BF),
            pltpu.VMEM((colours, 384, 640), BF),
            pltpu.VMEM((colours, 6, 32, 1024), BF),
            pltpu.VMEM((colours, 32, strip), F32),
            pltpu.VMEM((colours, 2, 32, strip), BF),
            pltpu.VMEM((colours, 2, 32, strip), BF),
            pltpu.VMEM((colours, 32, strip), BF),
            pltpu.VMEM((colours, 4, 32, strip), BF),
            pltpu.VMEM((colours, 3, 32, strip), BF),
            pltpu.VMEM((2, 384, strip), BF),
            pltpu.VMEM((384, 640), F32),
            pltpu.VMEM((24, 640), F32),
            pltpu.VMEM((16, 512), F32),
            pltpu.VMEM((2, 4, 384), F32),
            pltpu.VMEM((colours, 2, 16, 384), BF),
            pltpu.VMEM((colours, 2, caps, 16, 384), BF),
            pltpu.VMEM((colours, caps, 16, 512), F32),
            dma((6,)), dma((2,)), dma((2,)), dma((colours, 2)), dma((colours, 2)),
            dma((colours, banks)), dma((colours, banks)), dma((colours, 2)), dma((colours, 2)),
            dma((colours, 2, caps)), dma((colours, 2, caps)), dma((colours, caps)), dma((colours, caps)),
            pltpu.SemaphoreType.REGULAR,
        ],
        compiler_params=pltpu.CompilerParams(
            collective_id=0, has_side_effects=True, vmem_limit_bytes=62 << 20
        ),
    )(tile_patch, sat_tiles, measured, row_kernels, col_kernels, pattern)


def solution(mesh):
    return jax.shard_map(
        body,
        mesh=mesh,
        in_specs=(
            P("cap", None, None, "field"),
            P("cap", None, None, "field"),
            P("field", None, "bank", None),
            P("field", None, "bank", None),
            P("field"),
            P("cap", None),
        ),
        out_specs=(P("field", None, "bank", None), P("field", None, "bank", None)),
        check_vma=False,
    )
```
